32 devices in a mesh: groups: 2 (over y), tok: 4 (over z), cache: 2 (over x), rep: 2 (over core).
Axes of the slice: x: 2, y: 2, z: 4, core: 2. Of those that a mesh axis runs over, the one named last changes fastest.
Arguments:
- x_in: bfloat16 [16, 512, 8192], P(('groups', 'rep'), 'tok', 'cache'), parts along dimension 0, may hold values from -6 to 6
- z_in: bfloat16 [16, 512, 8192], P(('groups', 'rep'), 'tok', 'cache'), parts along dimension 0, may hold values from -6 to 6
- b_in: bfloat16 [16, 512, 8, 128], P(('groups', 'rep'), 'tok', 'cache'), parts along dimension 0, may hold values from -6 to 6
- c_in: bfloat16 [16, 512, 8, 128], P(('groups', 'rep'), 'tok', 'cache'), parts along dimension 0, may hold values from -6 to 6
- dt_in: bfloat16 [16, 512, 128], P(('groups', 'rep'), 'tok', 'cache'), parts along dimension 0, may hold values from -2 to 10
- dt_bias: float32 [128], P('cache'), may hold values from -14 to -2
- a_log: float32 [128], P('cache'), may hold values from 0 to 3
- skip_gain: float32 [128], P('cache'), may hold values from 0.5 to 1.5
- norm_w: float32 [8192], P('cache'), may hold values from 0.5 to 1.5
- cache_states: float32 [8, 2, 64, 64, 128], P(('groups', 'cache'), None, 'tok'), parts along dimension 0, may hold values from -0.3 to 0.3
- parent: int32 [16], P('groups'), parts along dimension 0, may hold values from 0 to 3
- state_dev: int32 [8], P('groups'), parts along dimension 0, may hold values from 0 to 1, as said below
- state_slot: int32 [8], P('groups'), parts along dimension 0, may hold values from 0 to 1
- spans: int32 [16], P('groups'), parts along dimension 0, may hold values from 1 to 4
Outputs:
- y_out: bfloat16 [16, 512, 8192], P(('groups', 'rep'), 'tok', 'cache'), parts along dimension 0
- final_states: float32 [16, 128, 64, 128], P(('groups', 'rep'), ('cache', 'tok')), parts along dimension 0
The draws below stay inside these ranges and needn't reach their ends.
There are 2 independent parts, one for each index of `groups`. The reference program is written for one: setup_inputs(seed, part) draws one part's arguments, and reference() takes and returns one part's arrays. A program takes and returns all parts, laid end to end along the dimension named above; an argument that names none is the same for every part. Nothing has to cross between parts.
Inputs may be any that keep to these rules, and one draw needn't show every extreme that they name: state_dev and state_slot together name every pair of a cache index and a slot exactly once.
All inputs are finite; a program needn't handle non-finite values.
Results may differ from the reference program's by a relative error of at most 0.0075.
Values may be sent and summed in bfloat16 or wider, within the bound.
A program may use at most 128 MiB of HBM per device.

```python
import math
import jax
import jax.numpy as jnp
import numpy as np
from jax import lax

HEADS = 128
HEAD_DIM = 64
STATE = 128
GROUPS = 8
SPAN = 128
SLOTS_DEV = 2
HOLDERS = 2
BATCH_QUERIES = 8
QUERY_EXTENT = 512
NCHUNK = 4
KEPT = 4


def per_head_rates(key):
    time_scale = jnp.exp(jax.random.uniform(jax.random.fold_in(key, 31), (HEADS,), jnp.float32, 0.0, math.log(16.0)))
    slow_share = 0.55
    is_slow = jax.random.uniform(jax.random.fold_in(key, 32), (HEADS,), jnp.float32) < slow_share
    spread_draw = jax.random.uniform(jax.random.fold_in(key, 33), (HEADS,), jnp.float32)
    slow_rate = 0.3 * jnp.exp(spread_draw * math.log(1.0 / 0.3)) / QUERY_EXTENT
    fast_rate = jnp.exp(spread_draw * math.log(2.5)) / 50.0
    head_rate = jnp.where(is_slow, slow_rate, fast_rate)
    return (time_scale, head_rate)


def draw_a_log(key, part):
    time_scale, head_rate = per_head_rates(key)
    return jnp.log(time_scale).astype(jnp.float32)


def draw_dt_bias(key, part):
    time_scale, head_rate = per_head_rates(key)
    return jnp.log(jnp.expm1(head_rate / time_scale)).astype(jnp.float32)


def draw_dt_in(key, part):
    full_shape = (BATCH_QUERIES, QUERY_EXTENT, HEADS)
    jitter = jnp.clip(0.5 * jax.random.normal(jax.random.fold_in(key, 41), full_shape, jnp.float32), -2.0, 2.0)
    spurt_index = jax.random.randint(jax.random.fold_in(key, 42), (BATCH_QUERIES, 2), 0, QUERY_EXTENT)
    flagged_entries = jnp.any(jnp.arange(QUERY_EXTENT)[None, :, None] == spurt_index[:, None, :], axis=2)
    raw_value = jitter + math.log(QUERY_EXTENT / 2.0) * flagged_entries.astype(jnp.float32)[:, :, None]
    return raw_value.astype(jnp.bfloat16)


def kept_places(key):
    shuffled = jax.random.permutation(jax.random.fold_in(key, 51), KEPT)
    return (shuffled // SLOTS_DEV, shuffled % SLOTS_DEV)


def draw_state_dev(key, part):
    return kept_places(key)[0].astype(jnp.int32)


def draw_state_slot(key, part):
    return kept_places(key)[1].astype(jnp.int32)


def draw_spans(key, part):
    drawn_counts = jax.random.randint(jax.random.fold_in(key, 61), (BATCH_QUERIES,), 1, NCHUNK + 1)
    longest = jax.random.randint(jax.random.fold_in(key, 62), (), 0, BATCH_QUERIES)
    return jnp.where(jnp.arange(BATCH_QUERIES) == longest, NCHUNK, drawn_counts).astype(jnp.int32)


def place_ends(values, key, least, largest):
    longest = values.shape.index(max(values.shape))
    spots = []
    for shift in (0, 1):
        where = [jax.random.randint(jax.random.fold_in(key, axis), (), 0, length) for axis, length in enumerate(values.shape)]
        where[longest] = (where[longest] + shift) % values.shape[longest]
        spots.append(tuple(where))
    return values.at[spots[0]].set(least).at[spots[1]].set(largest)


def levels(stream_key, extent, cuts, least, largest):
    loudness = 1.0
    for dim, shards_of in cuts:
        heights = jax.random.uniform(jax.random.fold_in(jax.random.fold_in(stream_key, 6), dim), (shards_of,), jnp.float32, least / len(cuts), largest / len(cuts))
        loudness = loudness * jnp.repeat(jnp.exp(heights), extent[dim] // shards_of).reshape((-1,) + (1,) * (len(extent) - 1 - dim))
    return loudness


def rank_table(amount, skew):
    weights = [(1 << 20) // math.isqrt(standing ** skew) + 1 for standing in range(1, amount + 1)]
    width = 1 + sum(weights) // (1 << 30)
    return np.cumsum(np.array([max(1, weight // width) for weight in weights]))


def ranked(rng, dims, number_of, lean):
    grid = rank_table(number_of, lean)
    pick = jax.random.randint(jax.random.fold_in(rng, 1), dims, 0, int(grid[number_of - 1]))
    rank = jnp.searchsorted(jnp.asarray(grid, jnp.int32), pick, side="right")
    return jax.random.permutation(jax.random.fold_in(rng, 2), number_of)[rank].astype(jnp.int32)


def noise(stream_key, extent, width, most, split=(), held_as=jnp.bfloat16):
    drawn = width * jax.random.normal(stream_key, extent, jnp.float32)
    if split:
        drawn = drawn * levels(stream_key, extent, split, -0.22, 0.18)
    return jnp.clip(drawn, -most, most).astype(held_as)


def setup_inputs(seed: int = 0, part: int = 0) -> dict:
    arg_keys = jax.random.split(jax.random.key(seed), 15)
    part_keys = jax.random.split(jax.random.fold_in(arg_keys[14], part), 15)
    return {
        "x_in": noise(part_keys[0], (BATCH_QUERIES, QUERY_EXTENT, HEADS * HEAD_DIM), 1.0, 6.0, ((0, 2), (1, 4), (2, 2))),
        "z_in": noise(part_keys[1], (BATCH_QUERIES, QUERY_EXTENT, HEADS * HEAD_DIM), 1.0, 6.0, ((0, 2), (1, 4), (2, 2))),
        "b_in": noise(part_keys[2], (BATCH_QUERIES, QUERY_EXTENT, GROUPS, STATE), 1.0, 6.0, ((0, 2), (1, 4), (2, 2))),
        "c_in": noise(part_keys[3], (BATCH_QUERIES, QUERY_EXTENT, GROUPS, STATE), 1.0, 6.0, ((0, 2), (1, 4), (2, 2))),
        "dt_in": draw_dt_in(jax.random.fold_in(jax.random.fold_in(arg_keys[14], part), 71), part),
        "dt_bias": draw_dt_bias(jax.random.fold_in(arg_keys[14], 71), part),
        "a_log": draw_a_log(jax.random.fold_in(arg_keys[14], 71), part),
        "skip_gain": jnp.clip(0.5 + 1.0 * jax.random.uniform(arg_keys[7], (HEADS,), jnp.float32) ** levels(arg_keys[7], (HEADS,), ((0, 2),), -0.2, 0.2), 0.5, 1.5),
        "norm_w": jnp.clip(1.0 + 0.1 * jax.random.normal(arg_keys[8], (HEADS * HEAD_DIM,), jnp.float32), 0.5, 1.5),
        "cache_states": noise(part_keys[9], (KEPT, HOLDERS, HEADS // HOLDERS, HEAD_DIM, STATE), 0.05, 0.3, ((0, 2), (2, 4)), jnp.float32),
        "parent": place_ends(ranked(part_keys[10], (BATCH_QUERIES,), KEPT, 2), jax.random.fold_in(part_keys[10], 3), 0, KEPT - 1).astype(jnp.int32),
        "state_dev": draw_state_dev(jax.random.fold_in(jax.random.fold_in(arg_keys[14], part), 71), part),
        "state_slot": draw_state_slot(jax.random.fold_in(jax.random.fold_in(arg_keys[14], part), 71), part),
        "spans": draw_spans(jax.random.fold_in(jax.random.fold_in(arg_keys[14], part), 71), part),
    }


EPS = 1e-05

def one_request(inputs, dt_bias, a_log, skip_gain, norm_w):
    x_row, z_row, b_row, c_row, raw_row, interval_total, initial = inputs
    head_count = raw_row.shape[1]
    groups = b_row.shape[1]
    per_group = head_count // groups
    blocks = QUERY_EXTENT // SPAN
    valid_mask = (jnp.arange(QUERY_EXTENT) < interval_total * SPAN).astype(jnp.float32)
    step_size = jax.nn.softplus(raw_row.astype(jnp.float32) + dt_bias) * valid_mask[:, None]
    step_blocks = step_size.reshape(blocks, SPAN, head_count).transpose(0, 2, 1)
    cum_rate = jnp.cumsum(-jnp.exp(a_log)[:, None] * step_blocks, axis=2)
    b_blocks = b_row.reshape(blocks, SPAN, groups, STATE).astype(jnp.float32)
    c_blocks = c_row.reshape(blocks, SPAN, groups, STATE).astype(jnp.float32)
    x_blocks = x_row.reshape(blocks, SPAN, head_count, HEAD_DIM).astype(jnp.float32)
    scores = jnp.repeat(jnp.einsum('kign,kjgn->kgij', c_blocks, b_blocks), per_group, axis=1)
    causal = jnp.arange(SPAN)[:, None] >= jnp.arange(SPAN)[None, :]
    spread = cum_rate[:, :, :, None] - cum_rate[:, :, None, :]
    decay_mask = jnp.where(causal, jnp.exp(jnp.where(causal, spread, 0.0)), 0.0)
    blend_factors = (scores * decay_mask * step_blocks[:, :, None, :]).astype(jnp.bfloat16)
    diagonal = jnp.einsum('khij,kjhp->kihp', blend_factors.astype(jnp.float32), x_blocks)
    weight = jnp.exp(cum_rate[:, :, -1:] - cum_rate) * step_blocks
    b_heads = jnp.repeat(b_blocks, per_group, axis=2)
    scaled = (b_heads * weight.transpose(0, 2, 1)[..., None]).astype(jnp.bfloat16)
    block_states = jnp.einsum('kjhp,kjhn->khpn', x_blocks, scaled.astype(jnp.float32))
    running_totals = cum_rate[:, :, -1]

    def advance(carried, step_inputs):
        block_total, new_state = step_inputs
        return (jnp.exp(block_total)[:, None, None] * carried + new_state, carried)
    final_state, before = lax.scan(advance, initial, (running_totals, block_states))
    before_grouped = before.reshape(blocks, groups, per_group, HEAD_DIM, STATE)
    carried_in = jnp.einsum('kign,kgepn->kigep', c_blocks, before_grouped, precision=lax.Precision.HIGHEST)
    carried_in = carried_in.reshape(blocks, SPAN, head_count, HEAD_DIM)
    growth = jnp.exp(cum_rate).transpose(0, 2, 1)[..., None]
    ssd = (diagonal + carried_in * growth + skip_gain[:, None] * x_blocks).astype(jnp.bfloat16)
    gated = ssd.reshape(QUERY_EXTENT, head_count * HEAD_DIM).astype(jnp.float32) * jax.nn.silu(z_row.astype(jnp.float32))
    grouped = gated.reshape(QUERY_EXTENT, groups, -1)
    inverse_rms = lax.rsqrt(lax.optimization_barrier(jnp.mean(grouped * grouped, axis=-1, keepdims=True)) + EPS)
    result = (grouped * inverse_rms).reshape(QUERY_EXTENT, -1) * norm_w * valid_mask[:, None]
    return (result.astype(jnp.bfloat16), final_state)

def reference(x_in, z_in, b_in, c_in, dt_in, dt_bias, a_log, skip_gain, norm_w, cache_states, parent, state_dev, state_slot, spans):
    kept_rows = state_dev[parent] * SLOTS_DEV + state_slot[parent]
    initial = cache_states[kept_rows].reshape(BATCH_QUERIES, HEADS, HEAD_DIM, STATE)

    def handle(inputs):
        return one_request(inputs, dt_bias, a_log, skip_gain, norm_w)
    y_out, final_states = lax.map(handle, (x_in, z_in, b_in, c_in, dt_in, spans, initial))
    return (y_out, final_states)
```

```python
import functools

import jax
import jax.numpy as jnp
from jax import lax
from jax.experimental import pallas as pl
from jax.experimental.pallas import tpu as pltpu
from jax.sharding import PartitionSpec as P

HEADS = 128
HEAD_DIM = 64
STATE = 128
GROUPS = 8
SPAN = 128
PER_GROUP = HEADS // GROUPS
WIDTH = PER_GROUP * HEAD_DIM
CHUNK = 256
EPS = 1e-05
MESH = pl.DeviceIdType.MESH
F32 = jnp.float32
BF16 = jnp.bfloat16


def contract(a, b, da, db, precision=None):
    return lax.dot_general(
        a, b, (((da,), (db,)), ((), ())), precision=precision, preferred_element_type=F32
    )


def scan_kernel(
    tok_n,
    cache_n,
    requests,
    groups,
    slots,
    parent,
    state_dev,
    state_slot,
    spans,
    step_t,
    rate_t,
    skip_w,
    norm_w,
    x_in,
    z_in,
    b_in,
    c_in,
    kept_in,
    y_out,
    final_out,
    kept_send,
    kept,
    initial,
    carry_in,
    carry_out,
    final_in,
    local_state,
    direct,
    columns,
    totals,
    expand,
    upper,
    gated,
    kx_send,
    kx_recv,
    init_send,
    init_recv,
    chain_send,
    chain_recv,
    fin_send,
    fin_recv,
):
    t = lax.axis_index("tok")
    c = lax.axis_index("cache")
    rep = lax.axis_index("rep")
    last = tok_n - 1
    units = requests * groups
    pieces = tok_n // groups
    rows = WIDTH // pieces

    barrier = pltpu.get_barrier_semaphore()
    for d in range(1, tok_n):
        pl.semaphore_signal(
            barrier, inc=1, device_id={"tok": lax.rem(t + d, tok_n)}, device_id_type=MESH
        )
    for d in range(1, cache_n):
        pl.semaphore_signal(
            barrier, inc=1, device_id={"cache": lax.rem(c + d, cache_n)}, device_id_type=MESH
        )

    for s in range(slots):
        for i in range(cache_n):
            kept_send[i * slots + s] = kept_in[s, i].astype(BF16)
        kept[c * slots + s] = kept_in[s, c].astype(BF16)

    pl.semaphore_wait(barrier, tok_n + cache_n - 2)

    def kept_copy(d):
        peer = lax.rem(c + d, cache_n)
        return pltpu.make_async_remote_copy(
            src_ref=kept_send.at[pl.ds(peer * slots, slots)],
            dst_ref=kept.at[pl.ds(c * slots, slots)],
            send_sem=kx_send.at[d - 1],
            recv_sem=kx_recv.at[d - 1],
            device_id={"cache": peer},
            device_id_type=MESH,
        )

    def init_copy(r, unit, piece, owner):
        return pltpu.make_async_remote_copy(
            src_ref=initial.at[r],
            dst_ref=carry_in.at[unit, pl.ds(pl.multiple_of(piece * rows, rows), rows)],
            send_sem=init_send.at[r],
            recv_sem=init_recv.at[r, owner],
            device_id={"tok": 0},
            device_id_type=MESH,
        )

    def chain_copy(unit):
        return pltpu.make_async_remote_copy(
            src_ref=carry_out.at[unit],
            dst_ref=carry_in.at[unit],
            send_sem=chain_send.at[unit],
            recv_sem=chain_recv.at[unit],
            device_id={"tok": lax.rem(t + 1, tok_n)},
            device_id_type=MESH,
        )

    def final_copy(r, unit, piece, owner):
        return pltpu.make_async_remote_copy(
            src_ref=carry_out.at[unit, pl.ds(pl.multiple_of(piece * rows, rows), rows)],
            dst_ref=final_in.at[r],
            send_sem=fin_send.at[r, owner],
            recv_sem=fin_recv.at[r],
            device_id={"tok": owner},
            device_id_type=MESH,
        )

    def place(u):
        others = groups - 1
        first = u < requests
        later = jnp.int32(0)
        for k in range(1, requests):
            later = later + jnp.where(u >= requests + k * others, 1, 0).astype(jnp.int32)
        r = jnp.where(first, u, later)
        g = jnp.where(first, 0, u + (1 - requests) - later * others)
        return r, g

    def unit_of(r, g):
        return jnp.where(g == 0, r, requests + r * (groups - 1) + g - 1)

    def valid_of(r):
        return jnp.where(t < spans[rep * requests + r], 1.0, 0.0).astype(F32)

    for d in range(1, cache_n):
        kept_copy(d).start()

    row_i = lax.broadcasted_iota(jnp.int32, (SPAN, SPAN), 0)
    col_i = lax.broadcasted_iota(jnp.int32, (SPAN, SPAN), 1)
    upper[...] = jnp.where(row_i <= col_i, 1.0, 0.0).astype(F32)
    e_row = lax.broadcasted_iota(jnp.int32, (SPAN, WIDTH), 0)
    e_col = lax.broadcasted_iota(jnp.int32, (SPAN, WIDTH), 1)
    same = (e_row & (PER_GROUP - 1)) == (e_col // HEAD_DIM)
    block = e_row // PER_GROUP
    expand[0] = jnp.where(same & ((block == 1) | (block == 2)), 1.0, 0.0).astype(BF16)
    expand[1] = jnp.where(same & ((block == 3) | (block == 4)), 1.0, 0.0).astype(BF16)

    def prepare(u):
        r, g = place(u)
        heads = pl.ds(pl.multiple_of(g * PER_GROUP, PER_GROUP), PER_GROUP)
        lanes = pl.ds(pl.multiple_of(g * STATE, STATE), STATE)
        step = step_t[r, heads, :] * valid_of(r)
        cum = contract(rate_t[heads, :] * step, upper[...], 1, 0, lax.Precision.HIGHEST)
        total = cum[:, SPAN - 1 :]
        weight = jnp.exp(total - cum) * step
        growth = jnp.exp(cum)
        weight_hi = weight.astype(BF16).astype(F32)
        growth_hi = growth.astype(BF16).astype(F32)
        stacked = jnp.concatenate(
            [
                cum,
                weight_hi,
                weight - weight_hi,
                growth_hi,
                growth - growth_hi,
                jnp.zeros((SPAN - 5 * PER_GROUP, SPAN), F32),
            ],
            axis=0,
        )
        turned = stacked.T
        split = turned.astype(BF16)
        columns[...] = split
        totals[...] = jnp.broadcast_to(jnp.exp(total), (PER_GROUP, STATE))
        b_block = b_in[r, :, lanes]
        c_block = c_in[r, :, lanes]
        for k in range(WIDTH // CHUNK):
            here = pl.ds(pl.multiple_of(g * WIDTH + k * CHUNK, CHUNK), CHUNK)
            wide = contract(split, expand[0, :, k * CHUNK : (k + 1) * CHUNK], 1, 0)
            scaled = (x_in[r, :, here].astype(F32) * wide).astype(BF16)
            local_state[k * CHUNK : (k + 1) * CHUNK, :] = contract(scaled, b_block, 0, 0)
        scores = contract(c_block, b_block, 1, 1)
        scores = jnp.where(row_i >= col_i, scores, 0.0)
        low = jnp.where(lax.broadcasted_iota(jnp.int32, (1, SPAN), 1) < HEAD_DIM, 1.0, 0.0)
        low_mask = low.astype(BF16)
        high_mask = (1.0 - low).astype(BF16)
        for k in range(PER_GROUP // 2):
            mixes = []
            for h in (2 * k, 2 * k + 1):
                spread = turned[:, h : h + 1] - cum[h : h + 1, :]
                mix = scores * jnp.exp(jnp.minimum(spread, 0.0)) * step[h : h + 1, :]
                mixes.append(mix.astype(BF16))
            here = pl.ds(pl.multiple_of(g * WIDTH + k * SPAN, SPAN), SPAN)
            x_pair = x_in[r, :, here]
            x_split = jnp.concatenate([x_pair * low_mask, x_pair * high_mask], axis=0)
            out = contract(jnp.concatenate(mixes, axis=1), x_split, 1, 0)
            direct[:, k * SPAN : (k + 1) * SPAN] = out + skip_w[:, here] * x_pair.astype(F32)

    def advance(u):
        r, g = place(u)
        if tok_n > 1:

            @pl.when(t > 0)
            def _():
                chain_copy(u).wait_recv()

            for q in range(pieces):
                owner = g * pieces + q

                @pl.when((t == 0) & (owner != 0))
                def _():
                    init_copy(r, u, q, owner).wait_recv()

        for h in range(PER_GROUP):
            part = slice(h * HEAD_DIM, (h + 1) * HEAD_DIM)
            carried = carry_in[u, part, :].astype(F32) * totals[h : h + 1, :]
            carry_out[u, part, :] = (carried + local_state[part, :]).astype(BF16)

        @pl.when(t < last)
        def _():
            chain_copy(u).start()

        for q in range(pieces):
            owner = g * pieces + q

            @pl.when((t == last) & (owner != last))
            def _():
                final_copy(r, u, q, owner).start()

            @pl.when((t == last) & (owner == last))
            def _():
                final_out[r] = carry_out[u, q * rows : (q + 1) * rows, :].astype(F32)

        lanes = pl.ds(pl.multiple_of(g * STATE, STATE), STATE)
        c_block = c_in[r, :, lanes]
        split = columns[...]
        power = jnp.zeros((SPAN, 1), F32)
        for k in range(WIDTH // CHUNK):
            part = slice(k * CHUNK, (k + 1) * CHUNK)
            here = pl.ds(pl.multiple_of(g * WIDTH + k * CHUNK, CHUNK), CHUNK)
            wide = contract(split, expand[1, :, part], 1, 0)
            carried = contract(c_block, carry_in[u, part, :], 1, 1)
            ssd = (direct[:, part] + carried * wide).astype(BF16).astype(F32)
            gate = z_in[r, :, here].astype(F32)
            value = ssd * (gate / (1.0 + jnp.exp(-gate)))
            gated[:, part] = value
            power = power + jnp.sum(value * value, axis=1, keepdims=True)
        inverse = lax.rsqrt(power * (1.0 / WIDTH) + EPS) * valid_of(r)
        for k in range(WIDTH // CHUNK):
            part = slice(k * CHUNK, (k + 1) * CHUNK)
            here = pl.ds(pl.multiple_of(g * WIDTH + k * CHUNK, CHUNK), CHUNK)
            y_out[r, :, here] = (gated[:, part] * inverse * norm_w[:, here]).astype(BF16)

    for d in range(1, cache_n):
        kept_copy(d).wait_recv()
    my_group = t // pieces
    my_piece = lax.rem(t, pieces)
    for r in range(requests):
        kept_id = parent[rep * requests + r]
        row = state_dev[kept_id] * slots + state_slot[kept_id]
        state = kept[row]

        @pl.when(t == 0)
        def _():
            carry_in[r, 0:rows, :] = state

        @pl.when(t > 0)
        def _():
            initial[r] = state
            init_copy(r, unit_of(r, my_group), my_piece, t).start()

    @pl.loop(0, units)
    def _(u):
        prepare(u)
        advance(u)

    @pl.when(t < last)
    def _():
        for r in range(requests):
            final_copy(r, unit_of(r, my_group), my_piece, t).wait_recv()
            final_out[r] = final_in[r].astype(F32)

        @pl.loop(0, units)
        def _(u):
            chain_copy(u).wait_send()

    @pl.when(t > 0)
    def _():
        for r in range(requests):
            init_copy(r, unit_of(r, my_group), my_piece, t).wait_send()

    @pl.when(t == last)
    def _():
        @pl.loop(0, units)
        def _(u):
            r, g = place(u)
            for q in range(pieces):
                owner = g * pieces + q

                @pl.when(owner != last)
                def _():
                    final_copy(r, u, q, owner).wait_send()

    for d in range(1, cache_n):
        kept_copy(d).wait_send()


def shards(
    x_in,
    z_in,
    b_in,
    c_in,
    dt_in,
    dt_bias,
    a_log,
    skip_gain,
    norm_w,
    cache_states,
    parent,
    state_dev,
    state_slot,
    spans,
):
    tok_n = lax.axis_size("tok")
    cache_n = lax.axis_size("cache")
    requests, segment, channels = x_in.shape
    groups = channels // WIDTH
    heads = groups * PER_GROUP
    slots = cache_states.shape[0]
    units = requests * groups
    owned = heads // tok_n * HEAD_DIM
    step_t = jax.nn.softplus(dt_in.astype(F32) + dt_bias).transpose(0, 2, 1)
    rate_t = jnp.broadcast_to(-jnp.exp(a_log)[:, None], (heads, SPAN))
    skip_w = jnp.repeat(skip_gain, HEAD_DIM)[None, :]
    vmem = pl.BlockSpec(memory_space=pltpu.VMEM)
    smem = pl.BlockSpec(memory_space=pltpu.SMEM)
    dma = pltpu.SemaphoreType.DMA
    y_out, final_states = pl.pallas_call(
        functools.partial(scan_kernel, tok_n, cache_n, requests, groups, slots),
        out_shape=(
            jax.ShapeDtypeStruct((requests, segment, channels), BF16),
            jax.ShapeDtypeStruct((requests, owned, STATE), F32),
        ),
        in_specs=[smem] * 4 + [vmem] * 9,
        out_specs=(vmem, vmem),
        scratch_shapes=[
            pltpu.VMEM((cache_n * slots, owned, STATE), BF16),
            pltpu.VMEM((cache_n * slots, owned, STATE), BF16),
            pltpu.VMEM((requests, owned, STATE), BF16),
            pltpu.VMEM((units, WIDTH, STATE), BF16),
            pltpu.VMEM((units, WIDTH, STATE), BF16),
            pltpu.VMEM((requests, owned, STATE), BF16),
            pltpu.VMEM((WIDTH, STATE), F32),
            pltpu.VMEM((SPAN, WIDTH), F32),
            pltpu.VMEM((SPAN, SPAN), BF16),
            pltpu.VMEM((PER_GROUP, STATE), F32),
            pltpu.VMEM((2, SPAN, WIDTH), BF16),
            pltpu.VMEM((SPAN, SPAN), F32),
            pltpu.VMEM((SPAN, WIDTH), F32),
            dma((max(cache_n - 1, 1),)),
            dma((max(cache_n - 1, 1),)),
            dma((requests,)),
            dma((requests, tok_n)),
            dma((units,)),
            dma((units,)),
            dma((requests, tok_n)),
            dma((requests,)),
        ],
        compiler_params=pltpu.CompilerParams(
            collective_id=0, has_side_effects=True, vmem_limit_bytes=60 * 1024 * 1024
        ),
        cost_estimate=pl.CostEstimate(
            flops=units * 14 * SPAN * SPAN * WIDTH,
            bytes_accessed=units * SPAN * WIDTH * 8,
            transcendentals=units * PER_GROUP * SPAN * SPAN,
        ),
    )(
        parent,
        state_dev,
        state_slot,
        spans,
        step_t,
        rate_t,
        skip_w,
        norm_w[None, :],
        x_in,
        z_in,
        b_in.reshape(requests, segment, groups * STATE),
        c_in.reshape(requests, segment, groups * STATE),
        cache_states.reshape(slots, cache_n, owned, STATE),
    )
    return (y_out, final_states.reshape(requests, heads // tok_n, HEAD_DIM, STATE))


def solution(mesh):
    placed = (
        P(("groups", "rep"), "tok", "cache"),
        P(("groups", "rep"), "tok", "cache"),
        P(("groups", "rep"), "tok", "cache", None),
        P(("groups", "rep"), "tok", "cache", None),
        P(("groups", "rep"), "tok", "cache"),
        P("cache"),
        P("cache"),
        P("cache"),
        P("cache"),
        P(("groups", "cache"), None, "tok", None, None),
        P("groups"),
        P("groups"),
        P("groups"),
        P("groups"),
    )
    return jax.shard_map(
        shards,
        mesh=mesh,
        in_specs=placed,
        out_specs=(
            P(("groups", "rep"), "tok", "cache"),
            P(("groups", "rep"), ("cache", "tok"), None, None),
        ),
        check_vma=False,
    )
```

```python
import functools

import jax
import jax.numpy as jnp
from jax import lax
from jax.experimental import pallas as pl
from jax.experimental.pallas import tpu as pltpu
from jax.sharding import PartitionSpec as P

HEADS = 128
HEAD_DIM = 64
STATE = 128
GROUPS = 8
SPAN = 128
PER_GROUP = HEADS // GROUPS
WIDTH = PER_GROUP * HEAD_DIM
CHUNK = 256
EPS = 1e-05
MESH = pl.DeviceIdType.MESH
F32 = jnp.float32
BF16 = jnp.bfloat16


def contract(a, b, da, db, precision=None):
    return lax.dot_general(
        a, b, (((da,), (db,)), ((), ())), precision=precision, preferred_element_type=F32
    )


def scan_kernel(
    tok_n,
    cache_n,
    requests,
    groups,
    slots,
    parent,
    state_dev,
    state_slot,
    spans,
    step_t,
    rate_t,
    skip_w,
    norm_w,
    x_in,
    z_in,
    b_in,
    c_in,
    kept_in,
    y_out,
    final_out,
    kept_send,
    kept,
    initial,
    carry_in,
    carry_out,
    final_in,
    local_state,
    direct,
    columns,
    totals,
    expand,
    upper,
    gated,
    kx_send,
    kx_recv,
    init_send,
    init_recv,
    chain_send,
    chain_recv,
    fin_send,
    fin_recv,
):
    t = lax.axis_index("tok")
    c = lax.axis_index("cache")
    rep = lax.axis_index("rep")
    last = tok_n - 1
    units = requests * groups
    pieces = tok_n // groups
    rows = WIDTH // pieces

    barrier = pltpu.get_barrier_semaphore()
    for d in range(1, tok_n):
        pl.semaphore_signal(
            barrier, inc=1, device_id={"tok": lax.rem(t + d, tok_n)}, device_id_type=MESH
        )
    for d in range(1, cache_n):
        pl.semaphore_signal(
            barrier, inc=1, device_id={"cache": lax.rem(c + d, cache_n)}, device_id_type=MESH
        )

    for s in range(slots):
        for i in range(cache_n):
            kept_send[i * slots + s] = kept_in[s, i].astype(BF16)
        kept[c * slots + s] = kept_in[s, c].astype(BF16)

    pl.semaphore_wait(barrier, tok_n + cache_n - 2)

    def kept_copy(d):
        peer = lax.rem(c + d, cache_n)
        return pltpu.make_async_remote_copy(
            src_ref=kept_send.at[pl.ds(peer * slots, slots)],
            dst_ref=kept.at[pl.ds(c * slots, slots)],
            send_sem=kx_send.at[d - 1],
            recv_sem=kx_recv.at[d - 1],
            device_id={"cache": peer},
            device_id_type=MESH,
        )

    def init_copy(r, unit, piece, owner):
        return pltpu.make_async_remote_copy(
            src_ref=initial.at[r],
            dst_ref=carry_in.at[unit, pl.ds(pl.multiple_of(piece * rows, rows), rows)],
            send_sem=init_send.at[r],
            recv_sem=init_recv.at[r, owner],
            device_id={"tok": 0},
            device_id_type=MESH,
        )

    def chain_copy(unit):
        return pltpu.make_async_remote_copy(
            src_ref=carry_out.at[unit],
            dst_ref=carry_in.at[unit],
            send_sem=chain_send.at[unit],
            recv_sem=chain_recv.at[unit],
            device_id={"tok": lax.rem(t + 1, tok_n)},
            device_id_type=MESH,
        )

    def final_copy(r, unit, piece, owner):
        return pltpu.make_async_remote_copy(
            src_ref=carry_out.at[unit, pl.ds(pl.multiple_of(piece * rows, rows), rows)],
            dst_ref=final_in.at[r],
            send_sem=fin_send.at[r, owner],
            recv_sem=fin_recv.at[r],
            device_id={"tok": owner},
            device_id_type=MESH,
        )

    def place(u):
        others = groups - 1
        first = u < requests
        later = jnp.int32(0)
        for k in range(1, requests):
            later = later + jnp.where(u >= requests + k * others, 1, 0).astype(jnp.int32)
        r = jnp.where(first, u, later)
        g = jnp.where(first, 0, u + (1 - requests) - later * others)
        return r, g

    def unit_of(r, g):
        return jnp.where(g == 0, r, requests + r * (groups - 1) + g - 1)

    def valid_of(r):
        return jnp.where(t < spans[rep * requests + r], 1.0, 0.0).astype(F32)

    for d in range(1, cache_n):
        kept_copy(d).start()

    row_i = lax.broadcasted_iota(jnp.int32, (SPAN, SPAN), 0)
    col_i = lax.broadcasted_iota(jnp.int32, (SPAN, SPAN), 1)
    upper[...] = jnp.where(row_i <= col_i, 1.0, 0.0).astype(F32)
    e_row = lax.broadcasted_iota(jnp.int32, (SPAN, WIDTH), 0)
    e_col = lax.broadcasted_iota(jnp.int32, (SPAN, WIDTH), 1)
    same = (e_row & (PER_GROUP - 1)) == (e_col // HEAD_DIM)
    block = e_row // PER_GROUP
    expand[0] = jnp.where(same & ((block == 1) | (block == 2)), 1.0, 0.0).astype(BF16)
    expand[1] = jnp.where(same & ((block == 3) | (block == 4)), 1.0, 0.0).astype(BF16)

    def prepare(u):
        r, g = place(u)
        heads = pl.ds(pl.multiple_of(g * PER_GROUP, PER_GROUP), PER_GROUP)
        lanes = pl.ds(pl.multiple_of(g * STATE, STATE), STATE)
        step = step_t[r, heads, :] * valid_of(r)
        cum = contract(rate_t[heads, :] * step, upper[...], 1, 0, lax.Precision.HIGHEST)
        total = cum[:, SPAN - 1 :]
        weight = jnp.exp(total - cum) * step
        growth = jnp.exp(cum)
        weight_hi = weight.astype(BF16).astype(F32)
        growth_hi = growth.astype(BF16).astype(F32)
        stacked = jnp.concatenate(
            [
                cum,
                weight_hi,
                weight - weight_hi,
                growth_hi,
                growth - growth_hi,
                jnp.zeros((SPAN - 5 * PER_GROUP, SPAN), F32),
            ],
            axis=0,
        )
        turned = stacked.T
        split = turned.astype(BF16)
        columns[...] = split
        totals[...] = jnp.broadcast_to(jnp.exp(total), (PER_GROUP, STATE))
        b_block = b_in[r, :, lanes]
        c_block = c_in[r, :, lanes]
        for k in range(WIDTH // CHUNK):
            here = pl.ds(pl.multiple_of(g * WIDTH + k * CHUNK, CHUNK), CHUNK)
            wide = contract(split, expand[0, :, k * CHUNK : (k + 1) * CHUNK], 1, 0)
            scaled = (x_in[r, :, here].astype(F32) * wide).astype(BF16)
            local_state[k * CHUNK : (k + 1) * CHUNK, :] = contract(scaled, b_block, 0, 0)
        scores = contract(c_block, b_block, 1, 1)
        scores = jnp.where(row_i >= col_i, scores, 0.0)
        low = jnp.where(lax.broadcasted_iota(jnp.int32, (1, SPAN), 1) < HEAD_DIM, 1.0, 0.0)
        low_mask = low.astype(BF16)
        high_mask = (1.0 - low).astype(BF16)
        for k in range(PER_GROUP // 2):
            mixes = []
            for h in (2 * k, 2 * k + 1):
                spread = turned[:, h : h + 1] - cum[h : h + 1, :]
                mix = scores * jnp.exp(jnp.minimum(spread, 0.0)) * step[h : h + 1, :]
                mixes.append(mix.astype(BF16))
            here = pl.ds(pl.multiple_of(g * WIDTH + k * SPAN, SPAN), SPAN)
            x_pair = x_in[r, :, here]
            x_split = jnp.concatenate([x_pair * low_mask, x_pair * high_mask], axis=0)
            out = contract(jnp.concatenate(mixes, axis=1), x_split, 1, 0)
            direct[:, k * SPAN : (k + 1) * SPAN] = out + skip_w[:, here] * x_pair.astype(F32)

    def advance(u):
        r, g = place(u)
        if tok_n > 1:

            @pl.when(t > 0)
            def _():
                chain_copy(u).wait_recv()

            for q in range(pieces):
                owner = g * pieces + q

                @pl.when((t == 0) & (owner != 0))
                def _():
                    init_copy(r, u, q, owner).wait_recv()

        for h in range(PER_GROUP):
            part = slice(h * HEAD_DIM, (h + 1) * HEAD_DIM)
            carried = carry_in[u, part, :].astype(F32) * totals[h : h + 1, :]
            carry_out[u, part, :] = (carried + local_state[part, :]).astype(BF16)

        @pl.when(t < last)
        def _():
            chain_copy(u).start()

        for q in range(pieces):
            owner = g * pieces + q

            @pl.when((t == last) & (owner != last))
            def _():
                final_copy(r, u, q, owner).start()

            @pl.when((t == last) & (owner == last))
            def _():
                final_out[r] = carry_out[u, q * rows : (q + 1) * rows, :].astype(F32)

        lanes = pl.ds(pl.multiple_of(g * STATE, STATE), STATE)
        c_block = c_in[r, :, lanes]
        split = columns[...]
        power = jnp.zeros((SPAN, 1), F32)
        for k in range(WIDTH // CHUNK):
            part = slice(k * CHUNK, (k + 1) * CHUNK)
            here = pl.ds(pl.multiple_of(g * WIDTH + k * CHUNK, CHUNK), CHUNK)
            wide = contract(split, expand[1, :, part], 1, 0)
            carried = contract(c_block, carry_in[u, part, :], 1, 1)
            ssd = (direct[:, part] + carried * wide).astype(BF16).astype(F32)
            gate = z_in[r, :, here].astype(F32)
            value = ssd * (gate / (1.0 + jnp.exp(-gate)))
            gated[:, part] = value
            power = power + jnp.sum(value * value, axis=1, keepdims=True)
        inverse = lax.rsqrt(power * (1.0 / WIDTH) + EPS) * valid_of(r)
        for k in range(WIDTH // CHUNK):
            part = slice(k * CHUNK, (k + 1) * CHUNK)
            here = pl.ds(pl.multiple_of(g * WIDTH + k * CHUNK, CHUNK), CHUNK)
            y_out[r, :, here] = (gated[:, part] * inverse * norm_w[:, here]).astype(BF16)

    for d in range(1, cache_n):
        kept_copy(d).wait_recv()
    sent_at = [(groups - 1) * r - 2 for r in range(requests)]
    my_group = t // pieces
    my_piece = lax.rem(t, pieces)
    for r in range(requests):
        kept_id = parent[rep * requests + r]
        row = state_dev[kept_id] * slots + state_slot[kept_id]
        state = kept[row]

        @pl.when(t == 0)
        def _():
            carry_in[r, 0:rows, :] = state

        @pl.when(t > 0)
        def _():
            initial[r] = state
            if sent_at[r] < 0:
                init_copy(r, unit_of(r, my_group), my_piece, t).start()

    @pl.loop(0, units)
    def _(u):
        for r in range(requests):
            if sent_at[r] >= 0:

                @pl.when((t > 0) & (u == sent_at[r]))
                def _():
                    init_copy(r, unit_of(r, my_group), my_piece, t).start()

        prepare(u)
        advance(u)

    @pl.when(t < last)
    def _():
        for r in range(requests):
            final_copy(r, unit_of(r, my_group), my_piece, t).wait_recv()
            final_out[r] = final_in[r].astype(F32)

        @pl.loop(0, units)
        def _(u):
            chain_copy(u).wait_send()

    @pl.when(t > 0)
    def _():
        for r in range(requests):
            init_copy(r, unit_of(r, my_group), my_piece, t).wait_send()

    @pl.when(t == last)
    def _():
        @pl.loop(0, units)
        def _(u):
            r, g = place(u)
            for q in range(pieces):
                owner = g * pieces + q

                @pl.when(owner != last)
                def _():
                    final_copy(r, u, q, owner).wait_send()

    for d in range(1, cache_n):
        kept_copy(d).wait_send()


def shards(
    x_in,
    z_in,
    b_in,
    c_in,
    dt_in,
    dt_bias,
    a_log,
    skip_gain,
    norm_w,
    cache_states,
    parent,
    state_dev,
    state_slot,
    spans,
):
    tok_n = lax.axis_size("tok")
    cache_n = lax.axis_size("cache")
    requests, segment, channels = x_in.shape
    groups = channels // WIDTH
    heads = groups * PER_GROUP
    slots = cache_states.shape[0]
    units = requests * groups
    owned = heads // tok_n * HEAD_DIM
    step_t = jax.nn.softplus(dt_in.astype(F32) + dt_bias).transpose(0, 2, 1)
    rate_t = jnp.broadcast_to(-jnp.exp(a_log)[:, None], (heads, SPAN))
    skip_w = jnp.repeat(skip_gain, HEAD_DIM)[None, :]
    vmem = pl.BlockSpec(memory_space=pltpu.VMEM)
    smem = pl.BlockSpec(memory_space=pltpu.SMEM)
    dma = pltpu.SemaphoreType.DMA
    y_out, final_states = pl.pallas_call(
        functools.partial(scan_kernel, tok_n, cache_n, requests, groups, slots),
        out_shape=(
            jax.ShapeDtypeStruct((requests, segment, channels), BF16),
            jax.ShapeDtypeStruct((requests, owned, STATE), F32),
        ),
        in_specs=[smem] * 4 + [vmem] * 9,
        out_specs=(vmem, vmem),
        scratch_shapes=[
            pltpu.VMEM((cache_n * slots, owned, STATE), BF16),
            pltpu.VMEM((cache_n * slots, owned, STATE), BF16),
            pltpu.VMEM((requests, owned, STATE), BF16),
            pltpu.VMEM((units, WIDTH, STATE), BF16),
            pltpu.VMEM((units, WIDTH, STATE), BF16),
            pltpu.VMEM((requests, owned, STATE), BF16),
            pltpu.VMEM((WIDTH, STATE), F32),
            pltpu.VMEM((SPAN, WIDTH), F32),
            pltpu.VMEM((SPAN, SPAN), BF16),
            pltpu.VMEM((PER_GROUP, STATE), F32),
            pltpu.VMEM((2, SPAN, WIDTH), BF16),
            pltpu.VMEM((SPAN, SPAN), F32),
            pltpu.VMEM((SPAN, WIDTH), F32),
            dma((max(cache_n - 1, 1),)),
            dma((max(cache_n - 1, 1),)),
            dma((requests,)),
            dma((requests, tok_n)),
            dma((units,)),
            dma((units,)),
            dma((requests, tok_n)),
            dma((requests,)),
        ],
        compiler_params=pltpu.CompilerParams(
            collective_id=0, has_side_effects=True, vmem_limit_bytes=60 * 1024 * 1024
        ),
        cost_estimate=pl.CostEstimate(
            flops=units * 14 * SPAN * SPAN * WIDTH,
            bytes_accessed=units * SPAN * WIDTH * 8,
            transcendentals=units * PER_GROUP * SPAN * SPAN,
        ),
    )(
        parent,
        state_dev,
        state_slot,
        spans,
        step_t,
        rate_t,
        skip_w,
        norm_w[None, :],
        x_in,
        z_in,
        b_in.reshape(requests, segment, groups * STATE),
        c_in.reshape(requests, segment, groups * STATE),
        cache_states.reshape(slots, cache_n, owned, STATE),
    )
    return (y_out, final_states.reshape(requests, heads // tok_n, HEAD_DIM, STATE))


def solution(mesh):
    placed = (
        P(("groups", "rep"), "tok", "cache"),
        P(("groups", "rep"), "tok", "cache"),
        P(("groups", "rep"), "tok", "cache", None),
        P(("groups", "rep"), "tok", "cache", None),
        P(("groups", "rep"), "tok", "cache"),
        P("cache"),
        P("cache"),
        P("cache"),
        P("cache"),
        P(("groups", "cache"), None, "tok", None, None),
        P("groups"),
        P("groups"),
        P("groups"),
        P("groups"),
    )
    return jax.shard_map(
        shards,
        mesh=mesh,
        in_specs=placed,
        out_specs=(
            P(("groups", "rep"), "tok", "cache"),
            P(("groups", "rep"), ("cache", "tok"), None, None),
        ),
        check_vma=False,
    )
```
